32 devices in a mesh: grp: 2 (over x), ep: 16 (over z, y, core).
Axes of the slice: x: 2, y: 2, z: 4, core: 2. Of those that a mesh axis runs over, the one named last changes fastest.
Arguments:
- tokens: bfloat16 [4096, 2048], P(('grp', 'ep')), parts along dimension 0, may hold values from -6 to 6
- cotangent: bfloat16 [4096, 2048], P(('grp', 'ep')), parts along dimension 0, may hold values from -18 to 18
- expert_ids: int32 [4096, 8], P(('grp', 'ep')), parts along dimension 0, may hold values from 0 to 15, all different within a row; in each aligned block of 128 rows (0 to 127, 128 to 255, ...) at most 72 rows name the same one
- routing: bfloat16 [4096, 8], P(('grp', 'ep')), parts along dimension 0, may hold values from 0.019897461 to 0.5
- gate_proj: bfloat16 [16, 2048, 384], P('ep'), may hold values from -0.125 to 0.125
- up_proj: bfloat16 [16, 2048, 384], P('ep'), may hold values from -0.125 to 0.125
- down_proj: bfloat16 [16, 384, 2048], P('ep'), may hold values from -0.3125 to 0.3125
Outputs:
- grad_tokens: bfloat16 [4096, 2048], P(('grp', 'ep')), parts along dimension 0
- grad_routing: bfloat16 [4096, 8], P(('grp', 'ep')), parts along dimension 0
- grad_gate: bfloat16 [32, 2048, 384], P(('grp', 'ep')), parts along dimension 0
- grad_up: bfloat16 [32, 2048, 384], P(('grp', 'ep')), parts along dimension 0
- grad_down: bfloat16 [32, 384, 2048], P(('grp', 'ep')), parts along dimension 0
The draws below stay inside these ranges and needn't reach their ends.
There are 2 independent parts, one for each index of `grp`. The reference program is written for one: setup_inputs(seed, part) draws one part's arguments, and reference() takes and returns one part's arrays. A program takes and returns all parts, laid end to end along the dimension named above; an argument that names none is the same for every part. Nothing has to cross between parts.
Inputs may be any that keep to these rules, and one draw needn't show every extreme that they name: `expert_ids`: each row names 8 different experts; among the 128 rows of one device no expert is named by more than 72 rows, a bound that some block reaches.
All inputs are finite; a program needn't handle non-finite values.
Results may differ from the reference program's by a relative error of at most 0.0058.
Values may be sent and summed in bfloat16 or wider, within the bound.
A program may use at most 128 MiB of HBM per device.

```python
import math
import jax
import jax.numpy as jnp
import numpy as np
from jax import lax

D = 2048
F = 384
TOP = 8
TOK_DEV = 128
EXPERTS = 16
TOKENS = 2048
MOST = 72
N_EP = 16


def steps_of(key, dims, shards, smallest, high):
    level, own = 1.0, jax.random.fold_in(key, 6)
    for axis_at, blocks in shards:
        heights = jnp.exp(jax.random.uniform(jax.random.fold_in(own, axis_at), (blocks,), jnp.float32, smallest / len(shards), high / len(shards)))
        level = level * jnp.repeat(heights, dims[axis_at] // blocks).reshape([-1 if axis == axis_at else 1 for axis in range(len(dims))])
    return level


def assign_block(rng, own, number, rows, count, top, most, slope):
    order = jax.random.permutation(rng, count)
    crowded, ordinary = shares(count, rows * top, most, slope, True), shares(count, rows * top, most, slope, False)
    places = jnp.arange(count)

    def named(tallies, rotation):
        used = int((tallies > 0).sum())
        fixed = max(1, used // 4)
        shifted = fixed + (places - fixed + rotation * (used - fixed)) % max(1, count - fixed)
        return jnp.zeros((count,), jnp.int32).at[order[jnp.where(places < fixed, places, shifted)]].set(jnp.asarray(tallies, jnp.int32))

    tallies = jnp.where(number % 4 == 0, named(crowded, number // 4), named(ordinary, number - number // 4 - 1))
    mixed = jax.random.permutation(jax.random.fold_in(own, 3), count)
    donor, taker = mixed[0:count // 2 * 2:2], mixed[1:count // 2 * 2:2]
    margin = jnp.minimum(tallies[donor] - 1, most - tallies[taker]) // 2
    margin = jnp.where((donor == order[0]) | (taker == order[0]) | (tallies[taker] == 0), 0, jnp.maximum(margin, 0))
    shifted = jax.random.randint(jax.random.fold_in(own, 4), (count // 2,), 0, 1 << 20) % (margin + 1)
    tallies = tallies.at[donor].add(-shifted).at[taker].add(shifted)
    labels = jnp.searchsorted(jnp.cumsum(tallies), jnp.arange(rows * top), side="right").astype(jnp.int32)
    grid = labels.reshape(top, rows).T
    grid = grid[jax.random.permutation(jax.random.fold_in(own, 1), rows)]
    rotation = jax.random.randint(jax.random.fold_in(own, 2), (rows, 1), 0, top)
    return jnp.take_along_axis(grid, (jnp.arange(top)[None, :] + rotation) % top, axis=1)


def shares(amount, total, most, slope, full):
    loads = [(1 << 20) // math.isqrt(grade ** slope) + 1 for grade in range(1, amount + 1)]
    largest = most if full else min(most, max(-(-total // amount), total * loads[0] // sum(loads)))
    least = 1 if total - largest >= amount - 1 else 0
    holding, spare = [largest] + [least] * (amount - 1), total - largest - least * (amount - 1)
    while spare > 0:
        movable = [i for i in range(1, amount) if holding[i] < largest] or [i for i in range(1, amount) if holding[i] < most]
        mass, budget = sum([loads[i] for i in movable]), spare
        for i in movable:
            more = min(most - holding[i], max(1, budget * loads[i] // mass), spare)
            holding[i] = holding[i] + more
            spare = spare - more
    return np.array(holding)


def noise(key, shape, scale, bound, cuts=(), kind=jnp.bfloat16):
    result = jax.random.normal(key, shape, jnp.float32) * scale
    if len(cuts) > 0:
        result = steps_of(key, shape, cuts, -0.22, 0.18) * result
    return jnp.clip(result, min=-bound, max=bound).astype(kind)


def setup_inputs(seed: int = 0, part: int = 0) -> dict:
    key_of = jax.random.split(jax.random.key(seed), 8)
    part_splits = jax.random.split(jax.random.fold_in(key_of[7], part), 8)
    tokens = noise(part_splits[0], (TOKENS, D), 1.0, 6.0, ((0, 16),))
    cotangent = noise(part_splits[1], (TOKENS, D), 3.0, 18.0, ((0, 16),))
    expert_ids_keys = jax.random.split(jax.random.fold_in(part_splits[2], 1), TOKENS // TOK_DEV)
    expert_ids_turns = jax.random.permutation(jax.random.fold_in(part_splits[2], 3), TOKENS // TOK_DEV)
    expert_ids = jax.vmap(lambda own, number: assign_block(jax.random.fold_in(part_splits[2], 2), own, number, TOK_DEV, EXPERTS, TOP, MOST, 2))(expert_ids_keys, expert_ids_turns).reshape((TOKENS, TOP))
    routing = jnp.clip(jnp.exp(math.log(0.5) - 3.224016 * jax.random.uniform(part_splits[3], (TOKENS, TOP), jnp.float32) ** steps_of(part_splits[3], (TOKENS, TOP), ((0, 16),), -0.2, 0.2)), 0.019897461, 0.5).astype(jnp.bfloat16)
    gate_proj = noise(key_of[4], (EXPERTS, D, F), D ** -0.5, 0.125, ((0, 16),))
    up_proj = noise(key_of[5], (EXPERTS, D, F), D ** -0.5, 0.125, ((0, 16),))
    down_proj = noise(key_of[6], (EXPERTS, F, D), F ** -0.5, 0.3125, ((0, 16),))
    return dict(tokens=tokens, cotangent=cotangent, expert_ids=expert_ids, routing=routing, gate_proj=gate_proj, up_proj=up_proj, down_proj=down_proj)


def expert_rows(rows_in, cotangent_rows, weight_in, gate_w, up_w, down_w):
    gate_pre = jnp.dot(rows_in, gate_w, preferred_element_type=jnp.float32)
    up_pre = jnp.dot(rows_in, up_w, preferred_element_type=jnp.float32)
    gate_sigmoid = jax.nn.sigmoid(gate_pre)
    activated = gate_pre * gate_sigmoid
    hidden = activated * up_pre
    hidden_raw = jnp.dot(cotangent_rows, down_w.T, preferred_element_type=jnp.float32)
    delta_prob = jnp.sum(hidden * hidden_raw, axis=-1).astype(jnp.bfloat16)
    scale_col = weight_in.astype(jnp.float32)[:, None]
    hidden_grad = scale_col * hidden_raw
    up_grad = (hidden_grad * activated).astype(jnp.bfloat16)
    gate_grad = (hidden_grad * up_pre * gate_sigmoid * (1.0 + gate_pre * (1.0 - gate_sigmoid))).astype(jnp.bfloat16)
    grad_rows = (jnp.dot(gate_grad, gate_w.T, preferred_element_type=jnp.float32)
                 + jnp.dot(up_grad, up_w.T, preferred_element_type=jnp.float32)).astype(jnp.bfloat16)
    scaled_hidden = (scale_col * hidden).astype(jnp.bfloat16)
    return grad_rows, delta_prob, gate_grad, up_grad, scaled_hidden


def reference(tokens, cotangent, expert_ids, routing, gate_proj, up_proj, down_proj):
    buffer_rows = N_EP * MOST
    per_device = expert_ids.reshape(N_EP, TOK_DEV * TOP)
    matches = (per_device[:, :, None] == jnp.arange(EXPERTS, dtype=jnp.int32)[None, None, :]).astype(jnp.int32)
    slot_index = jnp.sum((jnp.cumsum(matches, axis=1, dtype=jnp.int32) - matches) * matches, axis=2, dtype=jnp.int32)
    source = jnp.arange(N_EP, dtype=jnp.int32)[:, None]
    position = (source * MOST + slot_index).reshape(-1).astype(jnp.int32)
    flat_ids = expert_ids.reshape(-1).astype(jnp.int32)
    owner_row = (jnp.arange(TOKENS * TOP, dtype=jnp.int32) // TOP).astype(jnp.int32)
    row_table = jnp.full((EXPERTS, buffer_rows), TOKENS, jnp.int32).at[flat_ids, position].set(owner_row)
    weight_table = jnp.zeros((EXPERTS, buffer_rows), jnp.bfloat16).at[flat_ids, position].set(routing.reshape(-1))
    tokens_padded = jnp.concatenate([tokens, jnp.zeros((1, D), tokens.dtype)], axis=0)
    cotangent_padded = jnp.concatenate([cotangent, jnp.zeros((1, D), cotangent.dtype)], axis=0)

    def one_expert(pieces):
        table_row, weight_row, gate_w, up_w, down_w = pieces
        rows_in = tokens_padded[table_row]
        cotangent_rows = cotangent_padded[table_row]
        grad_rows, delta_prob, gate_grad, up_grad, scaled_hidden = expert_rows(
            rows_in, cotangent_rows, weight_row, gate_w, up_w, down_w)
        grad_gate = jnp.dot(rows_in.T, gate_grad, preferred_element_type=jnp.float32).astype(jnp.bfloat16)
        grad_up = jnp.dot(rows_in.T, up_grad, preferred_element_type=jnp.float32).astype(jnp.bfloat16)
        grad_down = jnp.dot(scaled_hidden.T, cotangent_rows, preferred_element_type=jnp.float32).astype(jnp.bfloat16)
        return grad_rows, delta_prob, grad_gate, grad_up, grad_down

    grad_buffer, prob_buffer, grad_gate, grad_up, grad_down = lax.map(
        one_expert, (row_table, weight_table, gate_proj, up_proj, down_proj))
    assignment_grad = grad_buffer[flat_ids, position].astype(jnp.float32).reshape(TOKENS, TOP, D)
    grad_tokens = jnp.sum(assignment_grad, axis=1).astype(jnp.bfloat16)
    grad_routing = prob_buffer[flat_ids, position].reshape(TOKENS, TOP)
    return grad_tokens, grad_routing, grad_gate, grad_up, grad_down
```

```python
import jax
import jax.numpy as jnp
from jax import lax
from jax.sharding import PartitionSpec as P


def contract_last(left, right):
    return lax.dot_general(
        left, right, (((1,), (1,)), ((), ())), preferred_element_type=jnp.float32
    )


def contract_first(left, right):
    return lax.dot_general(
        left, right, (((0,), (0,)), ((), ())), preferred_element_type=jnp.float32
    )


def expert_rows(rows_in, cotangent_rows, weight_in, gate_w, up_w, down_w):
    gate_pre = jnp.dot(rows_in, gate_w, preferred_element_type=jnp.float32)
    up_pre = jnp.dot(rows_in, up_w, preferred_element_type=jnp.float32)
    gate_sigmoid = jax.nn.sigmoid(gate_pre)
    activated = gate_pre * gate_sigmoid
    hidden = activated * up_pre
    hidden_raw = contract_last(cotangent_rows, down_w)
    delta_prob = jnp.sum(hidden * hidden_raw, axis=-1).astype(jnp.bfloat16)
    scale_col = weight_in.astype(jnp.float32)[:, None]
    hidden_grad = scale_col * hidden_raw
    up_grad = (hidden_grad * activated).astype(jnp.bfloat16)
    gate_grad = (
        hidden_grad * up_pre * gate_sigmoid * (1.0 + gate_pre * (1.0 - gate_sigmoid))
    ).astype(jnp.bfloat16)
    grad_rows = (contract_last(gate_grad, gate_w) + contract_last(up_grad, up_w)).astype(
        jnp.bfloat16
    )
    scaled_hidden = (scale_col * hidden).astype(jnp.bfloat16)
    return (grad_rows, delta_prob, gate_grad, up_grad, scaled_hidden)


def local(tokens, cotangent, expert_ids, routing, gate_proj, up_proj, down_proj):
    peers = lax.axis_size("ep")
    tok_rows, model_width = tokens.shape
    choose = expert_ids.shape[1]
    assigned = tok_rows * choose
    capacity = assigned // peers + max(1, assigned // (8 * peers))
    total_rows = peers * capacity
    flat_ids = expert_ids.reshape(-1)
    matches = (flat_ids[:, None] == jnp.arange(peers, dtype=jnp.int32)[None, :]).astype(jnp.int32)
    slot_index = jnp.sum(
        (jnp.cumsum(matches, axis=0, dtype=jnp.int32) - matches) * matches, axis=1, dtype=jnp.int32
    )
    target = flat_ids * capacity + slot_index
    owner_row = jnp.arange(assigned, dtype=jnp.int32) // choose
    send_rows = jnp.zeros((total_rows, model_width), jnp.bfloat16).at[target].set(tokens[owner_row])
    send_cotangent = (
        jnp.zeros((total_rows, model_width), jnp.bfloat16).at[target].set(cotangent[owner_row])
    )
    send_weight = jnp.zeros((total_rows,), jnp.bfloat16).at[target].set(routing.reshape(-1))
    send_rows = send_rows.reshape(peers, capacity, model_width)
    send_cotangent = send_cotangent.reshape(peers, capacity, model_width)
    send_weight = send_weight.reshape(peers, capacity)
    gate_w = gate_proj[0]
    up_w = up_proj[0]
    down_w = down_proj[0]
    hidden_width = gate_w.shape[1]
    rows_in = lax.all_to_all(send_rows, "ep", split_axis=0, concat_axis=0, tiled=True)
    cotangent_in = lax.all_to_all(send_cotangent, "ep", split_axis=0, concat_axis=0, tiled=True)
    weight_in = lax.all_to_all(send_weight, "ep", split_axis=0, concat_axis=0, tiled=True)
    count = rows_in.shape[1]
    grad_rows, delta_prob, gate_grad, up_grad, scaled_hidden = expert_rows(
        rows_in.reshape(-1, model_width),
        cotangent_in.reshape(-1, model_width),
        weight_in.reshape(-1),
        gate_w,
        up_w,
        down_w,
    )
    back_rows = lax.all_to_all(
        grad_rows.reshape(peers, count, model_width), "ep", split_axis=0, concat_axis=0, tiled=True
    )
    back_prob = lax.all_to_all(
        delta_prob.reshape(peers, count), "ep", split_axis=0, concat_axis=0, tiled=True
    )
    recv_rows, recv_cotangent, gate_grad, up_grad, scaled_hidden, back_rows, back_prob = (
        rows_in,
        cotangent_in,
        gate_grad.reshape(peers, count, hidden_width),
        up_grad.reshape(peers, count, hidden_width),
        scaled_hidden.reshape(peers, count, hidden_width),
        back_rows,
        back_prob,
    )
    inputs_all = recv_rows.reshape(total_rows, model_width)
    cotangent_all = recv_cotangent.reshape(total_rows, model_width)
    gate_grad = gate_grad.reshape(total_rows, hidden_width)
    up_grad = up_grad.reshape(total_rows, hidden_width)
    scaled_hidden = scaled_hidden.reshape(total_rows, hidden_width)
    grad_gate = contract_first(inputs_all, gate_grad).astype(jnp.bfloat16)[None]
    grad_up = contract_first(inputs_all, up_grad).astype(jnp.bfloat16)[None]
    grad_down = contract_first(scaled_hidden, cotangent_all).astype(jnp.bfloat16)[None]
    back_flat = back_rows.reshape(total_rows, model_width)
    assignment_grad = back_flat[target].astype(jnp.float32).reshape(tok_rows, choose, model_width)
    grad_tokens = jnp.sum(assignment_grad, axis=1).astype(jnp.bfloat16)
    grad_routing = back_prob.reshape(-1)[target].reshape(tok_rows, choose)
    return (grad_tokens, grad_routing, grad_gate, grad_up, grad_down)


def dense_local(tokens, cotangent, expert_ids, routing, gate_proj, up_proj, down_proj):
    peers = lax.axis_size("ep")
    tok_rows, model_width = tokens.shape
    experts = jnp.arange(peers, dtype=jnp.int32)
    chosen = expert_ids[:, None, :] == experts[None, :, None]
    weight = jnp.sum(
        jnp.where(chosen, routing.astype(jnp.float32)[:, None, :], 0.0), axis=2
    ).astype(jnp.bfloat16)
    weight_in = lax.all_to_all(weight.T, "ep", split_axis=0, concat_axis=0, tiled=True)
    rows_in = lax.all_gather(tokens, "ep", axis=0, tiled=True)
    cotangent_in = lax.all_gather(cotangent, "ep", axis=0, tiled=True)
    grad_rows, delta_prob, gate_grad, up_grad, scaled_hidden = expert_rows(
        rows_in, cotangent_in, weight_in.reshape(-1), gate_proj[0], up_proj[0], down_proj[0]
    )
    back_prob = lax.all_to_all(
        delta_prob.reshape(peers, tok_rows), "ep", split_axis=0, concat_axis=0, tiled=True
    )
    grad_tokens = lax.psum_scatter(grad_rows, "ep", scatter_dimension=0, tiled=True)
    grad_gate = contract_first(rows_in, gate_grad).astype(jnp.bfloat16)[None]
    grad_up = contract_first(rows_in, up_grad).astype(jnp.bfloat16)[None]
    grad_down = contract_first(scaled_hidden, cotangent_in).astype(jnp.bfloat16)[None]
    grad_routing = jnp.sum(
        jnp.where(chosen, back_prob.T.astype(jnp.float32)[:, :, None], 0.0), axis=1
    ).astype(jnp.bfloat16)
    return (grad_tokens, grad_routing, grad_gate, grad_up, grad_down)


def solution(mesh):
    return jax.shard_map(
        dense_local if mesh.shape["ep"] <= 16 else local,
        mesh=mesh,
        in_specs=(
            P(("grp", "ep"), None),
            P(("grp", "ep"), None),
            P(("grp", "ep"), None),
            P(("grp", "ep"), None),
            P("ep", None, None),
            P("ep", None, None),
            P("ep", None, None),
        ),
        out_specs=(
            P(("grp", "ep"), None),
            P(("grp", "ep"), None),
            P(("grp", "ep"), None, None),
            P(("grp", "ep"), None, None),
            P(("grp", "ep"), None, None),
        ),
        check_vma=False,
    )
```

```python
import functools

import jax
import jax.numpy as jnp
from jax import lax
from jax.experimental import pallas as pl
from jax.experimental.pallas import tpu as pltpu
from jax.sharding import PartitionSpec as P


def contract_last(left, right):
    return lax.dot_general(
        left, right, (((1,), (1,)), ((), ())), preferred_element_type=jnp.float32
    )


def contract_first(left, right):
    return lax.dot_general(
        left, right, (((0,), (0,)), ((), ())), preferred_element_type=jnp.float32
    )


def expert_rows(rows_in, cotangent_rows, weight_in, gate_w, up_w, down_w):
    gate_pre = jnp.dot(rows_in, gate_w, preferred_element_type=jnp.float32)
    up_pre = jnp.dot(rows_in, up_w, preferred_element_type=jnp.float32)
    gate_sigmoid = jax.nn.sigmoid(gate_pre)
    activated = gate_pre * gate_sigmoid
    hidden = activated * up_pre
    hidden_raw = contract_last(cotangent_rows, down_w)
    delta_prob = jnp.sum(hidden * hidden_raw, axis=-1).astype(jnp.bfloat16)
    scale_col = weight_in.astype(jnp.float32)[:, None]
    hidden_grad = scale_col * hidden_raw
    up_grad = (hidden_grad * activated).astype(jnp.bfloat16)
    gate_grad = (
        hidden_grad * up_pre * gate_sigmoid * (1.0 + gate_pre * (1.0 - gate_sigmoid))
    ).astype(jnp.bfloat16)
    grad_rows = (contract_last(gate_grad, gate_w) + contract_last(up_grad, up_w)).astype(
        jnp.bfloat16
    )
    scaled_hidden = (scale_col * hidden).astype(jnp.bfloat16)
    return (grad_rows, delta_prob, gate_grad, up_grad, scaled_hidden)


def local(tokens, cotangent, expert_ids, routing, gate_proj, up_proj, down_proj):
    peers = lax.axis_size("ep")
    tok_rows, model_width = tokens.shape
    choose = expert_ids.shape[1]
    assigned = tok_rows * choose
    capacity = assigned // peers + max(1, assigned // (8 * peers))
    total_rows = peers * capacity
    flat_ids = expert_ids.reshape(-1)
    matches = (flat_ids[:, None] == jnp.arange(peers, dtype=jnp.int32)[None, :]).astype(jnp.int32)
    slot_index = jnp.sum(
        (jnp.cumsum(matches, axis=0, dtype=jnp.int32) - matches) * matches, axis=1, dtype=jnp.int32
    )
    target = flat_ids * capacity + slot_index
    owner_row = jnp.arange(assigned, dtype=jnp.int32) // choose
    send_rows = jnp.zeros((total_rows, model_width), jnp.bfloat16).at[target].set(tokens[owner_row])
    send_cotangent = (
        jnp.zeros((total_rows, model_width), jnp.bfloat16).at[target].set(cotangent[owner_row])
    )
    send_weight = jnp.zeros((total_rows,), jnp.bfloat16).at[target].set(routing.reshape(-1))
    send_rows = send_rows.reshape(peers, capacity, model_width)
    send_cotangent = send_cotangent.reshape(peers, capacity, model_width)
    send_weight = send_weight.reshape(peers, capacity)
    gate_w = gate_proj[0]
    up_w = up_proj[0]
    down_w = down_proj[0]
    hidden_width = gate_w.shape[1]
    rows_in = lax.all_to_all(send_rows, "ep", split_axis=0, concat_axis=0, tiled=True)
    cotangent_in = lax.all_to_all(send_cotangent, "ep", split_axis=0, concat_axis=0, tiled=True)
    weight_in = lax.all_to_all(send_weight, "ep", split_axis=0, concat_axis=0, tiled=True)
    count = rows_in.shape[1]
    grad_rows, delta_prob, gate_grad, up_grad, scaled_hidden = expert_rows(
        rows_in.reshape(-1, model_width),
        cotangent_in.reshape(-1, model_width),
        weight_in.reshape(-1),
        gate_w,
        up_w,
        down_w,
    )
    back_rows = lax.all_to_all(
        grad_rows.reshape(peers, count, model_width), "ep", split_axis=0, concat_axis=0, tiled=True
    )
    back_prob = lax.all_to_all(
        delta_prob.reshape(peers, count), "ep", split_axis=0, concat_axis=0, tiled=True
    )
    recv_rows, recv_cotangent, gate_grad, up_grad, scaled_hidden, back_rows, back_prob = (
        rows_in,
        cotangent_in,
        gate_grad.reshape(peers, count, hidden_width),
        up_grad.reshape(peers, count, hidden_width),
        scaled_hidden.reshape(peers, count, hidden_width),
        back_rows,
        back_prob,
    )
    inputs_all = recv_rows.reshape(total_rows, model_width)
    cotangent_all = recv_cotangent.reshape(total_rows, model_width)
    gate_grad = gate_grad.reshape(total_rows, hidden_width)
    up_grad = up_grad.reshape(total_rows, hidden_width)
    scaled_hidden = scaled_hidden.reshape(total_rows, hidden_width)
    grad_gate = contract_first(inputs_all, gate_grad).astype(jnp.bfloat16)[None]
    grad_up = contract_first(inputs_all, up_grad).astype(jnp.bfloat16)[None]
    grad_down = contract_first(scaled_hidden, cotangent_all).astype(jnp.bfloat16)[None]
    back_flat = back_rows.reshape(total_rows, model_width)
    assignment_grad = back_flat[target].astype(jnp.float32).reshape(tok_rows, choose, model_width)
    grad_tokens = jnp.sum(assignment_grad, axis=1).astype(jnp.bfloat16)
    grad_routing = back_prob.reshape(-1)[target].reshape(tok_rows, choose)
    return (grad_tokens, grad_routing, grad_gate, grad_up, grad_down)


LANES = 128


def pick(table, row, column):
    value = jnp.int32(0)
    for r, entries in enumerate(table):
        for s, entry in enumerate(entries):
            value = value + jnp.where((row == r) & (column == s), entry, 0)
    return value


def expert_kernel(
    depth,
    first_rows,
    tokens_ref,
    cotangent_ref,
    ids_ref,
    routing_ref,
    gate_hbm,
    up_hbm,
    down_hbm,
    grad_tokens_ref,
    grad_routing_ref,
    grad_pair_ref,
    grad_down_ref,
    rows_all,
    partial,
    core_in,
    side_in,
    rise_in,
    fall_in,
    pair_t,
    hidden_t,
    gate_w,
    up_w,
    down_w,
    local_sem,
    gather_send,
    gather_recv,
    core_send,
    core_recv,
    side_send,
    side_recv,
    chain_send,
    chain_recv,
):
    block, width = tokens_ref.shape
    hidden_width = gate_w.shape[1]
    me = lax.axis_index("ep")
    z, y, c = me // 4, (me // 2) % 2, me % 2
    sibling = z * 4 + y * 2 + (1 - c)
    side = z * 4 + (1 - y) * 2 + c
    above, below = me + 4, me - 4
    near = [sorted(range(depth), key=lambda o, r=r: (abs(o - r), o)) for r in range(depth)]
    chain = [
        list(range(r + 1, depth)) + list(range(r - 1, -1, -1))
        if r < depth // 2
        else list(range(r - 1, -1, -1)) + list(range(r + 1, depth))
        for r in range(depth)
    ]
    parts = ((0, first_rows), (first_rows, block - first_rows))

    def at_rows(o, n=1):
        return pl.ds(pl.multiple_of(o * block, block), n * block)

    def local_copies():
        mine = at_rows(me)
        return (
            pltpu.make_async_copy(tokens_ref, rows_all.at[mine, 0:width], local_sem.at[0]),
            pltpu.make_async_copy(
                cotangent_ref, rows_all.at[mine, width : 2 * width], local_sem.at[1]
            ),
            pltpu.make_async_copy(gate_hbm, gate_w, local_sem.at[2]),
            pltpu.make_async_copy(up_hbm, up_w, local_sem.at[3]),
            pltpu.make_async_copy(down_hbm, down_w, local_sem.at[4]),
        )

    def gather_copy(kind, o, way, target):
        start, size = parts[kind]
        where = rows_all.at[pl.ds(pl.multiple_of(o * block + start, 16), size), :]
        return pltpu.make_async_remote_copy(
            src_ref=where,
            dst_ref=where,
            send_sem=gather_send.at[kind, way, o],
            recv_sem=gather_recv.at[kind, o],
            device_id={"ep": target},
            device_id_type=pl.DeviceIdType.MESH,
        )

    def send_along(kind, zo, o):
        @pl.when((zo <= z) & (z < depth - 1))
        def _():
            gather_copy(kind, o, 0, above).start()

        @pl.when((zo >= z) & (z > 0))
        def _():
            gather_copy(kind, o, 1, below).start()

    def arrive(kind, o):
        gather_copy(kind, o, 3, sibling).wait_recv()

    def forward(s):
        zo = pick(near, z, s)
        own = zo * 4 + y * 2 + c
        other = zo * 4 + (1 - y) * 2 + c

        @pl.when(s > 0)
        def _():
            arrive(0, own)

        send_along(0, zo, own)
        gather_copy(0, own, 2, side).start()

        @pl.when(s > 0)
        def _():
            arrive(1, own)

        send_along(1, zo, own)

        @pl.when(s == 0)
        def _():
            gather_copy(1, own, 2, side).start()

        gather_copy(0, own, 3, sibling).start()
        gather_copy(1, own, 3, sibling).start()
        arrive(1, other)
        send_along(1, zo, other)
        gather_copy(1, other, 3, sibling).start()

    def core_copy(zo, yo):
        return pltpu.make_async_remote_copy(
            src_ref=partial.at[at_rows(zo * 4 + yo * 2 + (1 - c)), :],
            dst_ref=core_in.at[at_rows(zo * 2 + yo), :],
            send_sem=core_send.at[zo * 2 + yo],
            recv_sem=core_recv.at[zo * 2 + yo],
            device_id={"ep": sibling},
            device_id_type=pl.DeviceIdType.MESH,
        )

    def side_copy(zo):
        return pltpu.make_async_remote_copy(
            src_ref=partial.at[at_rows(zo * 4 + (1 - y) * 2 + c), :],
            dst_ref=side_in.at[at_rows(zo), :],
            send_sem=side_send.at[zo],
            recv_sem=side_recv.at[zo],
            device_id={"ep": side},
            device_id_type=pl.DeviceIdType.MESH,
        )

    def chain_copy(zo, way, target):
        return pltpu.make_async_remote_copy(
            src_ref=partial.at[at_rows(zo * 4 + y * 2 + c), :],
            dst_ref=(rise_in if way == 0 else fall_in).at[at_rows(zo), :],
            send_sem=chain_send.at[way, zo],
            recv_sem=chain_recv.at[way, zo],
            device_id={"ep": target},
            device_id_type=pl.DeviceIdType.MESH,
        )

    def add_into(o, source, at):
        total = partial[at_rows(o), :].astype(jnp.float32) + source[at_rows(at), :].astype(
            jnp.float32
        )
        partial[at_rows(o), :] = total.astype(jnp.bfloat16)

    def compute(s):
        zo = pick(near, z, s)
        other = zo * 4 + (1 - y) * 2 + c
        arrive(0, other)
        gather_copy(0, other, 3, sibling).start()
        for kind in (0, 1):
            for yo in (0, 1):
                arrive(kind, zo * 4 + yo * 2 + (1 - c))

        @pl.when(s == 0)
        def _():
            for copy in local_copies()[2:]:
                copy.wait()

        @pl.loop(0, 2)
        def _(yo):
            start = pl.multiple_of((zo * 4 + yo * 2) * block, 2 * block)
            rows = pl.ds(start, 2 * block)
            lane = lax.broadcasted_iota(jnp.int32, (2 * block, LANES), 1)
            x = rows_all[rows, 0:width]
            gate_pre = jnp.dot(x, gate_w[...], preferred_element_type=jnp.float32)
            up_pre = jnp.dot(x, up_w[...], preferred_element_type=jnp.float32)
            hidden_raw = contract_last(rows_all[rows, width : 2 * width], down_w[...])
            weights = rows_all[rows, 2 * width : 2 * width + LANES].astype(jnp.float32)
            scale_col = jnp.sum(jnp.where(lane == me, weights, 0.0), axis=1, keepdims=True)
            gate_sigmoid = jax.nn.sigmoid(gate_pre)
            activated = gate_pre * gate_sigmoid
            hidden = activated * up_pre
            delta_prob = jnp.sum(hidden * hidden_raw, axis=1, keepdims=True)
            partial[rows, width : width + LANES] = jnp.where(lane == me, delta_prob, 0.0).astype(
                jnp.bfloat16
            )
            hidden_grad = scale_col * hidden_raw
            up_grad = hidden_grad * activated
            gate_grad = (
                hidden_grad * up_pre * gate_sigmoid * (1.0 + gate_pre * (1.0 - gate_sigmoid))
            )
            pair_t[0:hidden_width, rows] = gate_grad.T.astype(jnp.bfloat16)
            pair_t[hidden_width : 2 * hidden_width, rows] = up_grad.T.astype(jnp.bfloat16)
            hidden_t[:, rows] = (scale_col * hidden).T.astype(jnp.bfloat16)
            up_grad = up_grad.astype(jnp.bfloat16)
            gate_grad = gate_grad.astype(jnp.bfloat16)
            for tile in range(0, width, 512):
                span = slice(tile, tile + 512)
                partial[rows, span] = (
                    contract_last(gate_grad, gate_w[span, :])
                    + contract_last(up_grad, up_w[span, :])
                ).astype(jnp.bfloat16)
            core_copy(zo, yo).start()

    def sum_core(s):
        zo = pick(near, z, s)
        core_copy(zo, 1 - y).wait_recv()
        add_into(zo * 4 + (1 - y) * 2 + c, core_in, zo * 2 + (1 - y))
        side_copy(zo).start()
        core_copy(zo, y).wait_recv()
        add_into(zo * 4 + y * 2 + c, core_in, zo * 2 + y)

    def sum_side(s):
        zo = pick(near, z, s)
        side_copy(zo).wait_recv()
        add_into(zo * 4 + y * 2 + c, side_in, zo)

    def sum_chain(s):
        zo = pick(chain, z, s)
        own = zo * 4 + y * 2 + c

        @pl.when(zo > z)
        def _():
            @pl.when(z > 0)
            def _():
                chain_copy(zo, 0, above).wait_recv()
                add_into(own, rise_in, zo)

            chain_copy(zo, 0, above).start()

        @pl.when(zo < z)
        def _():
            @pl.when(z < depth - 1)
            def _():
                chain_copy(zo, 1, below).wait_recv()
                add_into(own, fall_in, zo)

            chain_copy(zo, 1, below).start()

    tile_width = 256

    def weight_grads(low, high):
        @pl.loop(low, high)
        def _(tile):
            start = pl.multiple_of(tile * tile_width, tile_width)
            span = pl.ds(start, tile_width)
            grad_pair_ref[:, span] = jnp.dot(
                pair_t[...], rows_all[:, span], preferred_element_type=jnp.float32
            ).astype(jnp.bfloat16)
            grad_down_ref[:, span] = jnp.dot(
                hidden_t[...],
                rows_all[:, pl.ds(pl.multiple_of(start + width, tile_width), tile_width)],
                preferred_element_type=jnp.float32,
            ).astype(jnp.bfloat16)

    for copy in local_copies():
        copy.start()
    barrier = pltpu.get_barrier_semaphore()
    for target in (sibling, side):
        pl.semaphore_signal(
            barrier, inc=1, device_id={"ep": target}, device_id_type=pl.DeviceIdType.MESH
        )

    @pl.when(z < depth - 1)
    def _():
        pl.semaphore_signal(
            barrier, inc=1, device_id={"ep": above}, device_id_type=pl.DeviceIdType.MESH
        )

    @pl.when(z > 0)
    def _():
        pl.semaphore_signal(
            barrier, inc=1, device_id={"ep": below}, device_id_type=pl.DeviceIdType.MESH
        )

    ends = jnp.where(z > 0, 1, 0) + jnp.where(z < depth - 1, 1, 0)
    pl.semaphore_wait(barrier, 2 + ends)
    lane = lax.broadcasted_iota(jnp.int32, (block, LANES), 1)
    choose = ids_ref.shape[1]
    weights = jnp.zeros((block, LANES), jnp.float32)
    for k in range(choose):
        weights = weights + jnp.where(
            lane == ids_ref[:, k : k + 1], routing_ref[:, k : k + 1].astype(jnp.float32), 0.0
        )
    rows_all[at_rows(me), 2 * width : 2 * width + LANES] = weights.astype(jnp.bfloat16)
    for copy in local_copies()[:2]:
        copy.wait()

    last = depth - 1

    @pl.loop(0, depth + 3)
    def _(s):
        @pl.when(s < depth)
        def _():
            forward(s)

        @pl.when((s >= 1) & (s <= depth))
        def _():
            compute(s - 1)

        @pl.when((s >= 2) & (s <= depth + 1))
        def _():
            sum_core(s - 2)

        @pl.when(s >= 3)
        def _():
            sum_side(s - 3)

        @pl.when(s == depth + 1)
        def _():
            sum_chain(0)
            weight_grads(0, 5)

    sum_chain(1)
    weight_grads(5, 6)
    for s in range(2, last):
        sum_chain(s)
    weight_grads(6, width // tile_width)

    @pl.when(z > 0)
    def _():
        chain_copy(z, 0, above).wait_recv()

    @pl.when(z == 0)
    def _():
        rise_in[at_rows(z), :] = jnp.zeros((block, width + LANES), jnp.bfloat16)

    @pl.when(z < depth - 1)
    def _():
        chain_copy(z, 1, below).wait_recv()

    @pl.when(z == depth - 1)
    def _():
        fall_in[at_rows(z), :] = jnp.zeros((block, width + LANES), jnp.bfloat16)

    total = (
        partial[at_rows(me), :].astype(jnp.float32)
        + rise_in[at_rows(z), :].astype(jnp.float32)
        + fall_in[at_rows(z), :].astype(jnp.float32)
    )
    grad_tokens_ref[...] = total[:, :width].astype(jnp.bfloat16)
    probs = total[:, width:]
    found = jnp.zeros((block, LANES), jnp.float32)
    for k in range(choose):
        value = jnp.sum(
            jnp.where(lane == ids_ref[:, k : k + 1], probs, 0.0), axis=1, keepdims=True
        )
        found = found + jnp.where(lane == k, value, 0.0)
    grad_routing_ref[...] = found.astype(jnp.bfloat16)

    @pl.loop(0, depth)
    def _(zo):
        own = zo * 4 + y * 2 + c
        other = zo * 4 + (1 - y) * 2 + c
        for kind, o in ((0, own), (1, own), (1, other)):
            @pl.when((zo <= z) & (z < depth - 1))
            def _(kind=kind, o=o):
                gather_copy(kind, o, 0, above).wait_send()

            @pl.when((zo >= z) & (z > 0))
            def _(kind=kind, o=o):
                gather_copy(kind, o, 1, below).wait_send()

        gather_copy(0, own, 2, side).wait_send()

        @pl.when(zo == z)
        def _():
            gather_copy(1, own, 2, side).wait_send()

        for kind in (0, 1):
            for o in (own, other):
                gather_copy(kind, o, 3, sibling).wait_send()
        core_copy(zo, 0).wait_send()
        core_copy(zo, 1).wait_send()
        side_copy(zo).wait_send()

        @pl.when(zo > z)
        def _():
            chain_copy(zo, 0, above).wait_send()

        @pl.when(zo < z)
        def _():
            chain_copy(zo, 1, below).wait_send()


def dense_local(tokens, cotangent, expert_ids, routing, gate_proj, up_proj, down_proj):
    peers = lax.axis_size("ep")
    depth = peers // 4
    block, width = tokens.shape
    choose = expert_ids.shape[1]
    hidden_width = gate_proj.shape[2]
    total = peers * block
    first_rows = block * 5 // 8
    bf16 = jnp.bfloat16
    vmem = pl.BlockSpec(memory_space=pltpu.VMEM)
    anywhere = pl.BlockSpec(memory_space=pl.ANY)
    dma = pltpu.SemaphoreType.DMA
    grad_tokens, grad_routing, grad_pair, grad_down = pl.pallas_call(
        functools.partial(expert_kernel, depth, first_rows),
        out_shape=(
            jax.ShapeDtypeStruct((block, width), bf16),
            jax.ShapeDtypeStruct((block, LANES), bf16),
            jax.ShapeDtypeStruct((2 * hidden_width, width), bf16),
            jax.ShapeDtypeStruct((hidden_width, width), bf16),
        ),
        in_specs=[anywhere, anywhere, vmem, vmem, anywhere, anywhere, anywhere],
        out_specs=(vmem, vmem, vmem, vmem),
        scratch_shapes=[
            pltpu.VMEM((total, 2 * width + LANES), bf16),
            pltpu.VMEM((total, width + LANES), bf16),
            pltpu.VMEM((total // 2, width + LANES), bf16),
            pltpu.VMEM((total // 4, width + LANES), bf16),
            pltpu.VMEM((total // 4, width + LANES), bf16),
            pltpu.VMEM((total // 4, width + LANES), bf16),
            pltpu.VMEM((2 * hidden_width, total), bf16),
            pltpu.VMEM((hidden_width, total), bf16),
            pltpu.VMEM((width, hidden_width), bf16),
            pltpu.VMEM((width, hidden_width), bf16),
            pltpu.VMEM((hidden_width, width), bf16),
            dma((5,)),
            dma((2, 4, peers)),
            dma((2, peers)),
            dma((2 * depth,)),
            dma((2 * depth,)),
            dma((depth,)),
            dma((depth,)),
            dma((2, depth)),
            dma((2, depth)),
        ],
        compiler_params=pltpu.CompilerParams(
            collective_id=0, has_side_effects=True, vmem_limit_bytes=62 << 20
        ),
        cost_estimate=pl.CostEstimate(
            flops=16 * total * width * hidden_width,
            bytes_accessed=20 * width * hidden_width,
            transcendentals=total * hidden_width,
        ),
    )(tokens, cotangent, expert_ids, routing, gate_proj[0], up_proj[0], down_proj[0])
    grad_pair = grad_pair.reshape(2, hidden_width, width)
    return (
        grad_tokens,
        grad_routing[:, :choose],
        grad_pair[:1].transpose(0, 2, 1),
        grad_pair[1:].transpose(0, 2, 1),
        grad_down[None],
    )


def solution(mesh):
    return jax.shard_map(
        dense_local if mesh.shape["ep"] == 16 else local,
        mesh=mesh,
        in_specs=(
            P(("grp", "ep"), None),
            P(("grp", "ep"), None),
            P(("grp", "ep"), None),
            P(("grp", "ep"), None),
            P("ep", None, None),
            P("ep", None, None),
            P("ep", None, None),
        ),
        out_specs=(
            P(("grp", "ep"), None),
            P(("grp", "ep"), None),
            P(("grp", "ep"), None, None),
            P(("grp", "ep"), None, None),
            P(("grp", "ep"), None, None),
        ),
        check_vma=False,
    )
```

```python
import functools

import jax
import jax.numpy as jnp
from jax import lax
from jax.experimental import pallas as pl
from jax.experimental.pallas import tpu as pltpu
from jax.sharding import PartitionSpec as P


def contract_last(left, right):
    return lax.dot_general(
        left, right, (((1,), (1,)), ((), ())), preferred_element_type=jnp.float32
    )


def contract_first(left, right):
    return lax.dot_general(
        left, right, (((0,), (0,)), ((), ())), preferred_element_type=jnp.float32
    )


def expert_rows(rows_in, cotangent_rows, weight_in, gate_w, up_w, down_w):
    gate_pre = jnp.dot(rows_in, gate_w, preferred_element_type=jnp.float32)
    up_pre = jnp.dot(rows_in, up_w, preferred_element_type=jnp.float32)
    gate_sigmoid = jax.nn.sigmoid(gate_pre)
    activated = gate_pre * gate_sigmoid
    hidden = activated * up_pre
    hidden_raw = contract_last(cotangent_rows, down_w)
    delta_prob = jnp.sum(hidden * hidden_raw, axis=-1).astype(jnp.bfloat16)
    scale_col = weight_in.astype(jnp.float32)[:, None]
    hidden_grad = scale_col * hidden_raw
    up_grad = (hidden_grad * activated).astype(jnp.bfloat16)
    gate_grad = (
        hidden_grad * up_pre * gate_sigmoid * (1.0 + gate_pre * (1.0 - gate_sigmoid))
    ).astype(jnp.bfloat16)
    grad_rows = (contract_last(gate_grad, gate_w) + contract_last(up_grad, up_w)).astype(
        jnp.bfloat16
    )
    scaled_hidden = (scale_col * hidden).astype(jnp.bfloat16)
    return (grad_rows, delta_prob, gate_grad, up_grad, scaled_hidden)


def local(tokens, cotangent, expert_ids, routing, gate_proj, up_proj, down_proj):
    peers = lax.axis_size("ep")
    tok_rows, model_width = tokens.shape
    choose = expert_ids.shape[1]
    assigned = tok_rows * choose
    capacity = assigned // peers + max(1, assigned // (8 * peers))
    total_rows = peers * capacity
    flat_ids = expert_ids.reshape(-1)
    matches = (flat_ids[:, None] == jnp.arange(peers, dtype=jnp.int32)[None, :]).astype(jnp.int32)
    slot_index = jnp.sum(
        (jnp.cumsum(matches, axis=0, dtype=jnp.int32) - matches) * matches, axis=1, dtype=jnp.int32
    )
    target = flat_ids * capacity + slot_index
    owner_row = jnp.arange(assigned, dtype=jnp.int32) // choose
    send_rows = jnp.zeros((total_rows, model_width), jnp.bfloat16).at[target].set(tokens[owner_row])
    send_cotangent = (
        jnp.zeros((total_rows, model_width), jnp.bfloat16).at[target].set(cotangent[owner_row])
    )
    send_weight = jnp.zeros((total_rows,), jnp.bfloat16).at[target].set(routing.reshape(-1))
    send_rows = send_rows.reshape(peers, capacity, model_width)
    send_cotangent = send_cotangent.reshape(peers, capacity, model_width)
    send_weight = send_weight.reshape(peers, capacity)
    gate_w = gate_proj[0]
    up_w = up_proj[0]
    down_w = down_proj[0]
    hidden_width = gate_w.shape[1]
    rows_in = lax.all_to_all(send_rows, "ep", split_axis=0, concat_axis=0, tiled=True)
    cotangent_in = lax.all_to_all(send_cotangent, "ep", split_axis=0, concat_axis=0, tiled=True)
    weight_in = lax.all_to_all(send_weight, "ep", split_axis=0, concat_axis=0, tiled=True)
    count = rows_in.shape[1]
    grad_rows, delta_prob, gate_grad, up_grad, scaled_hidden = expert_rows(
        rows_in.reshape(-1, model_width),
        cotangent_in.reshape(-1, model_width),
        weight_in.reshape(-1),
        gate_w,
        up_w,
        down_w,
    )
    back_rows = lax.all_to_all(
        grad_rows.reshape(peers, count, model_width), "ep", split_axis=0, concat_axis=0, tiled=True
    )
    back_prob = lax.all_to_all(
        delta_prob.reshape(peers, count), "ep", split_axis=0, concat_axis=0, tiled=True
    )
    recv_rows, recv_cotangent, gate_grad, up_grad, scaled_hidden, back_rows, back_prob = (
        rows_in,
        cotangent_in,
        gate_grad.reshape(peers, count, hidden_width),
        up_grad.reshape(peers, count, hidden_width),
        scaled_hidden.reshape(peers, count, hidden_width),
        back_rows,
        back_prob,
    )
    inputs_all = recv_rows.reshape(total_rows, model_width)
    cotangent_all = recv_cotangent.reshape(total_rows, model_width)
    gate_grad = gate_grad.reshape(total_rows, hidden_width)
    up_grad = up_grad.reshape(total_rows, hidden_width)
    scaled_hidden = scaled_hidden.reshape(total_rows, hidden_width)
    grad_gate = contract_first(inputs_all, gate_grad).astype(jnp.bfloat16)[None]
    grad_up = contract_first(inputs_all, up_grad).astype(jnp.bfloat16)[None]
    grad_down = contract_first(scaled_hidden, cotangent_all).astype(jnp.bfloat16)[None]
    back_flat = back_rows.reshape(total_rows, model_width)
    assignment_grad = back_flat[target].astype(jnp.float32).reshape(tok_rows, choose, model_width)
    grad_tokens = jnp.sum(assignment_grad, axis=1).astype(jnp.bfloat16)
    grad_routing = back_prob.reshape(-1)[target].reshape(tok_rows, choose)
    return (grad_tokens, grad_routing, grad_gate, grad_up, grad_down)


LANES = 128


def pick(table, row, column):
    value = jnp.int32(0)
    for r, entries in enumerate(table):
        for s, entry in enumerate(entries):
            value = value + jnp.where((row == r) & (column == s), entry, 0)
    return value


def expert_kernel(
    depth,
    first_rows,
    tokens_ref,
    cotangent_ref,
    ids_ref,
    routing_ref,
    gate_hbm,
    up_hbm,
    down_hbm,
    grad_tokens_ref,
    grad_routing_ref,
    grad_pair_ref,
    grad_down_ref,
    rows_all,
    partial,
    core_in,
    side_in,
    rise_in,
    fall_in,
    pair_t,
    hidden_t,
    gate_w,
    up_w,
    down_w,
    local_sem,
    gather_send,
    gather_recv,
    core_send,
    core_recv,
    side_send,
    side_recv,
    chain_send,
    chain_recv,
):
    block, width = tokens_ref.shape
    hidden_width = gate_w.shape[1]
    me = lax.axis_index("ep")
    z, y, c = me // 4, (me // 2) % 2, me % 2
    sibling = z * 4 + y * 2 + (1 - c)
    side = z * 4 + (1 - y) * 2 + c
    above, below = me + 4, me - 4
    near = [sorted(range(depth), key=lambda o, r=r: (abs(o - r), o)) for r in range(depth)]
    chain = [
        list(range(r + 1, depth)) + list(range(r - 1, -1, -1))
        if r < depth // 2
        else list(range(r - 1, -1, -1)) + list(range(r + 1, depth))
        for r in range(depth)
    ]
    parts = ((0, first_rows), (first_rows, block - first_rows))

    def at_rows(o, n=1):
        return pl.ds(pl.multiple_of(o * block, block), n * block)

    def local_copies():
        mine = at_rows(me)
        return (
            pltpu.make_async_copy(tokens_ref, rows_all.at[mine, 0:width], local_sem.at[0]),
            pltpu.make_async_copy(
                cotangent_ref, rows_all.at[mine, width : 2 * width], local_sem.at[1]
            ),
            pltpu.make_async_copy(gate_hbm, gate_w, local_sem.at[2]),
            pltpu.make_async_copy(up_hbm, up_w, local_sem.at[3]),
            pltpu.make_async_copy(down_hbm, down_w, local_sem.at[4]),
        )

    def gather_copy(kind, o, way, target):
        start, size = parts[kind]
        where = rows_all.at[pl.ds(pl.multiple_of(o * block + start, 16), size), :]
        return pltpu.make_async_remote_copy(
            src_ref=where,
            dst_ref=where,
            send_sem=gather_send.at[kind, way, o],
            recv_sem=gather_recv.at[kind, o],
            device_id={"ep": target},
            device_id_type=pl.DeviceIdType.MESH,
        )

    def send_along(kind, zo, o):
        @pl.when((zo <= z) & (z < depth - 1))
        def _():
            gather_copy(kind, o, 0, above).start()

        @pl.when((zo >= z) & (z > 0))
        def _():
            gather_copy(kind, o, 1, below).start()

    def arrive(kind, o):
        gather_copy(kind, o, 3, sibling).wait_recv()

    def forward(s):
        zo = pick(near, z, s)
        own = zo * 4 + y * 2 + c
        other = zo * 4 + (1 - y) * 2 + c

        @pl.when(s > 0)
        def _():
            arrive(0, own)

        send_along(0, zo, own)
        gather_copy(0, own, 2, side).start()

        @pl.when(s > 0)
        def _():
            arrive(1, own)

        send_along(1, zo, own)

        @pl.when(s == 0)
        def _():
            gather_copy(1, own, 2, side).start()

        gather_copy(0, own, 3, sibling).start()
        gather_copy(1, own, 3, sibling).start()
        arrive(1, other)
        send_along(1, zo, other)
        gather_copy(1, other, 3, sibling).start()

    def core_copy(zo, yo):
        return pltpu.make_async_remote_copy(
            src_ref=partial.at[at_rows(zo * 4 + yo * 2 + (1 - c)), :],
            dst_ref=core_in.at[at_rows(zo * 2 + yo), :],
            send_sem=core_send.at[zo * 2 + yo],
            recv_sem=core_recv.at[zo * 2 + yo],
            device_id={"ep": sibling},
            device_id_type=pl.DeviceIdType.MESH,
        )

    def side_copy(zo):
        return pltpu.make_async_remote_copy(
            src_ref=partial.at[at_rows(zo * 4 + (1 - y) * 2 + c), :],
            dst_ref=side_in.at[at_rows(zo), :],
            send_sem=side_send.at[zo],
            recv_sem=side_recv.at[zo],
            device_id={"ep": side},
            device_id_type=pl.DeviceIdType.MESH,
        )

    def half_rows(o, half):
        start = o * block + half * (block // 2)
        return pl.ds(pl.multiple_of(start, block // 2), block // 2)

    def chain_copy(zo, way, target, half):
        return pltpu.make_async_remote_copy(
            src_ref=partial.at[half_rows(zo * 4 + y * 2 + c, half), :],
            dst_ref=(rise_in if way == 0 else fall_in).at[half_rows(zo, half), :],
            send_sem=chain_send.at[way, zo, half],
            recv_sem=chain_recv.at[way, zo, half],
            device_id={"ep": target},
            device_id_type=pl.DeviceIdType.MESH,
        )

    def add_into(o, source, at):
        total = partial[at_rows(o), :].astype(jnp.float32) + source[at_rows(at), :].astype(
            jnp.float32
        )
        partial[at_rows(o), :] = total.astype(jnp.bfloat16)

    def compute(s):
        zo = pick(near, z, s)
        other = zo * 4 + (1 - y) * 2 + c
        arrive(0, other)
        gather_copy(0, other, 3, sibling).start()
        for kind in (0, 1):
            for yo in (0, 1):
                arrive(kind, zo * 4 + yo * 2 + (1 - c))

        @pl.when(s == 0)
        def _():
            for copy in local_copies()[2:]:
                copy.wait()

        @pl.loop(0, 2)
        def _(yo):
            start = pl.multiple_of((zo * 4 + yo * 2) * block, 2 * block)
            rows = pl.ds(start, 2 * block)
            lane = lax.broadcasted_iota(jnp.int32, (2 * block, LANES), 1)
            x = rows_all[rows, 0:width]
            gate_pre = jnp.dot(x, gate_w[...], preferred_element_type=jnp.float32)
            up_pre = jnp.dot(x, up_w[...], preferred_element_type=jnp.float32)
            hidden_raw = contract_last(rows_all[rows, width : 2 * width], down_w[...])
            weights = rows_all[rows, 2 * width : 2 * width + LANES].astype(jnp.float32)
            scale_col = jnp.sum(jnp.where(lane == me, weights, 0.0), axis=1, keepdims=True)
            gate_sigmoid = jax.nn.sigmoid(gate_pre)
            activated = gate_pre * gate_sigmoid
            hidden = activated * up_pre
            delta_prob = jnp.sum(hidden * hidden_raw, axis=1, keepdims=True)
            partial[rows, width : width + LANES] = jnp.where(lane == me, delta_prob, 0.0).astype(
                jnp.bfloat16
            )
            hidden_grad = scale_col * hidden_raw
            up_grad = hidden_grad * activated
            gate_grad = (
                hidden_grad * up_pre * gate_sigmoid * (1.0 + gate_pre * (1.0 - gate_sigmoid))
            )
            pair_t[0:hidden_width, rows] = gate_grad.T.astype(jnp.bfloat16)
            pair_t[hidden_width : 2 * hidden_width, rows] = up_grad.T.astype(jnp.bfloat16)
            hidden_t[:, rows] = (scale_col * hidden).T.astype(jnp.bfloat16)
            up_grad = up_grad.astype(jnp.bfloat16)
            gate_grad = gate_grad.astype(jnp.bfloat16)
            for tile in range(0, width, 512):
                span = slice(tile, tile + 512)
                partial[rows, span] = (
                    contract_last(gate_grad, gate_w[span, :])
                    + contract_last(up_grad, up_w[span, :])
                ).astype(jnp.bfloat16)
            core_copy(zo, yo).start()

    def sum_core(s):
        zo = pick(near, z, s)
        core_copy(zo, 1 - y).wait_recv()
        add_into(zo * 4 + (1 - y) * 2 + c, core_in, zo * 2 + (1 - y))
        side_copy(zo).start()
        core_copy(zo, y).wait_recv()
        add_into(zo * 4 + y * 2 + c, core_in, zo * 2 + y)

    def sum_side(s):
        zo = pick(near, z, s)
        side_copy(zo).wait_recv()
        add_into(zo * 4 + y * 2 + c, side_in, zo)

    def sum_chain(s):
        zo = pick(chain, z, s)
        own = zo * 4 + y * 2 + c

        def pass_on(way, target, inner, source):
            @pl.loop(0, 2)
            def _(half):
                @pl.when(inner)
                def _():
                    chain_copy(zo, way, target, half).wait_recv()
                    rows = half_rows(own, half)
                    total = partial[rows, :].astype(jnp.float32) + source[
                        half_rows(zo, half), :
                    ].astype(jnp.float32)
                    partial[rows, :] = total.astype(jnp.bfloat16)

                chain_copy(zo, way, target, half).start()

        @pl.when(zo > z)
        def _():
            pass_on(0, above, z > 0, rise_in)

        @pl.when(zo < z)
        def _():
            pass_on(1, below, z < depth - 1, fall_in)

    tile_width = 256

    def weight_grads(low, high):
        @pl.loop(low, high)
        def _(tile):
            start = pl.multiple_of(tile * tile_width, tile_width)
            span = pl.ds(start, tile_width)
            grad_pair_ref[:, span] = jnp.dot(
                pair_t[...], rows_all[:, span], preferred_element_type=jnp.float32
            ).astype(jnp.bfloat16)
            grad_down_ref[:, span] = jnp.dot(
                hidden_t[...],
                rows_all[:, pl.ds(pl.multiple_of(start + width, tile_width), tile_width)],
                preferred_element_type=jnp.float32,
            ).astype(jnp.bfloat16)

    for copy in local_copies():
        copy.start()
    barrier = pltpu.get_barrier_semaphore()
    for target in (sibling, side):
        pl.semaphore_signal(
            barrier, inc=1, device_id={"ep": target}, device_id_type=pl.DeviceIdType.MESH
        )

    @pl.when(z < depth - 1)
    def _():
        pl.semaphore_signal(
            barrier, inc=1, device_id={"ep": above}, device_id_type=pl.DeviceIdType.MESH
        )

    @pl.when(z > 0)
    def _():
        pl.semaphore_signal(
            barrier, inc=1, device_id={"ep": below}, device_id_type=pl.DeviceIdType.MESH
        )

    ends = jnp.where(z > 0, 1, 0) + jnp.where(z < depth - 1, 1, 0)
    pl.semaphore_wait(barrier, 2 + ends)
    lane = lax.broadcasted_iota(jnp.int32, (block, LANES), 1)
    choose = ids_ref.shape[1]
    weights = jnp.zeros((block, LANES), jnp.float32)
    for k in range(choose):
        weights = weights + jnp.where(
            lane == ids_ref[:, k : k + 1], routing_ref[:, k : k + 1].astype(jnp.float32), 0.0
        )
    rows_all[at_rows(me), 2 * width : 2 * width + LANES] = weights.astype(jnp.bfloat16)
    for copy in local_copies()[:2]:
        copy.wait()

    edge = (z == 0) | (z == depth - 1)
    last = depth - 1

    @pl.loop(0, depth + 2)
    def _(s):
        @pl.when(s < depth)
        def _():
            forward(s)

        @pl.when((s >= 1) & (s <= depth))
        def _():
            compute(s - 1)
            sum_core(s - 1)

        @pl.when(s == depth)
        def _():
            weight_grads(0, 4)

        @pl.when(s >= 2)
        def _():
            sum_side(s - 2)

        @pl.when((s >= 3) & edge)
        def _():
            sum_chain(s - 3)

        @pl.when((s == depth) & (z > 0) & (z < last))
        def _():
            sum_chain(0)

    @pl.when((z > 0) & (z < last))
    def _():
        @pl.loop(1, last)
        def _(s):
            sum_chain(s)

    weight_grads(4, width // tile_width)

    @pl.when(z > 0)
    def _():
        chain_copy(z, 0, above, 0).wait_recv()
        chain_copy(z, 0, above, 1).wait_recv()

    @pl.when(z == 0)
    def _():
        rise_in[at_rows(z), :] = jnp.zeros((block, width + LANES), jnp.bfloat16)

    @pl.when(z < depth - 1)
    def _():
        chain_copy(z, 1, below, 0).wait_recv()
        chain_copy(z, 1, below, 1).wait_recv()

    @pl.when(z == depth - 1)
    def _():
        fall_in[at_rows(z), :] = jnp.zeros((block, width + LANES), jnp.bfloat16)

    total = (
        partial[at_rows(me), :].astype(jnp.float32)
        + rise_in[at_rows(z), :].astype(jnp.float32)
        + fall_in[at_rows(z), :].astype(jnp.float32)
    )
    grad_tokens_ref[...] = total[:, :width].astype(jnp.bfloat16)
    probs = total[:, width:]
    found = jnp.zeros((block, LANES), jnp.float32)
    for k in range(choose):
        value = jnp.sum(
            jnp.where(lane == ids_ref[:, k : k + 1], probs, 0.0), axis=1, keepdims=True
        )
        found = found + jnp.where(lane == k, value, 0.0)
    grad_routing_ref[...] = found.astype(jnp.bfloat16)

    @pl.loop(0, depth)
    def _(zo):
        own = zo * 4 + y * 2 + c
        other = zo * 4 + (1 - y) * 2 + c
        for kind, o in ((0, own), (1, own), (1, other)):
            @pl.when((zo <= z) & (z < depth - 1))
            def _(kind=kind, o=o):
                gather_copy(kind, o, 0, above).wait_send()

            @pl.when((zo >= z) & (z > 0))
            def _(kind=kind, o=o):
                gather_copy(kind, o, 1, below).wait_send()

        gather_copy(0, own, 2, side).wait_send()

        @pl.when(zo == z)
        def _():
            gather_copy(1, own, 2, side).wait_send()

        for kind in (0, 1):
            for o in (own, other):
                gather_copy(kind, o, 3, sibling).wait_send()
        core_copy(zo, 0).wait_send()
        core_copy(zo, 1).wait_send()
        side_copy(zo).wait_send()

        @pl.when(zo > z)
        def _():
            chain_copy(zo, 0, above, 0).wait_send()
            chain_copy(zo, 0, above, 1).wait_send()

        @pl.when(zo < z)
        def _():
            chain_copy(zo, 1, below, 0).wait_send()
            chain_copy(zo, 1, below, 1).wait_send()


def dense_local(tokens, cotangent, expert_ids, routing, gate_proj, up_proj, down_proj):
    peers = lax.axis_size("ep")
    depth = peers // 4
    block, width = tokens.shape
    choose = expert_ids.shape[1]
    hidden_width = gate_proj.shape[2]
    total = peers * block
    first_rows = block * 6 // 8
    bf16 = jnp.bfloat16
    vmem = pl.BlockSpec(memory_space=pltpu.VMEM)
    anywhere = pl.BlockSpec(memory_space=pl.ANY)
    dma = pltpu.SemaphoreType.DMA
    grad_tokens, grad_routing, grad_pair, grad_down = pl.pallas_call(
        functools.partial(expert_kernel, depth, first_rows),
        out_shape=(
            jax.ShapeDtypeStruct((block, width), bf16),
            jax.ShapeDtypeStruct((block, LANES), bf16),
            jax.ShapeDtypeStruct((2 * hidden_width, width), bf16),
            jax.ShapeDtypeStruct((hidden_width, width), bf16),
        ),
        in_specs=[anywhere, anywhere, vmem, vmem, anywhere, anywhere, anywhere],
        out_specs=(vmem, vmem, vmem, vmem),
        scratch_shapes=[
            pltpu.VMEM((total, 2 * width + LANES), bf16),
            pltpu.VMEM((total, width + LANES), bf16),
            pltpu.VMEM((total // 2, width + LANES), bf16),
            pltpu.VMEM((total // 4, width + LANES), bf16),
            pltpu.VMEM((total // 4, width + LANES), bf16),
            pltpu.VMEM((total // 4, width + LANES), bf16),
            pltpu.VMEM((2 * hidden_width, total), bf16),
            pltpu.VMEM((hidden_width, total), bf16),
            pltpu.VMEM((width, hidden_width), bf16),
            pltpu.VMEM((width, hidden_width), bf16),
            pltpu.VMEM((hidden_width, width), bf16),
            dma((5,)),
            dma((2, 4, peers)),
            dma((2, peers)),
            dma((2 * depth,)),
            dma((2 * depth,)),
            dma((depth,)),
            dma((depth,)),
            dma((2, depth, 2)),
            dma((2, depth, 2)),
        ],
        compiler_params=pltpu.CompilerParams(
            collective_id=0, has_side_effects=True, vmem_limit_bytes=62 << 20
        ),
        cost_estimate=pl.CostEstimate(
            flops=16 * total * width * hidden_width,
            bytes_accessed=20 * width * hidden_width,
            transcendentals=total * hidden_width,
        ),
    )(tokens, cotangent, expert_ids, routing, gate_proj[0], up_proj[0], down_proj[0])
    grad_pair = grad_pair.reshape(2, hidden_width, width)
    return (
        grad_tokens,
        grad_routing[:, :choose],
        grad_pair[:1].transpose(0, 2, 1),
        grad_pair[1:].transpose(0, 2, 1),
        grad_down[None],
    )


def solution(mesh):
    return jax.shard_map(
        dense_local if mesh.shape["ep"] == 16 else local,
        mesh=mesh,
        in_specs=(
            P(("grp", "ep"), None),
            P(("grp", "ep"), None),
            P(("grp", "ep"), None),
            P(("grp", "ep"), None),
            P("ep", None, None),
            P("ep", None, None),
            P("ep", None, None),
        ),
        out_specs=(
            P(("grp", "ep"), None),
            P(("grp", "ep"), None),
            P(("grp", "ep"), None, None),
            P(("grp", "ep"), None, None),
            P(("grp", "ep"), None, None),
        ),
        check_vma=False,
    )
```

```python
import functools

import jax
import jax.numpy as jnp
from jax import lax
from jax.experimental import pallas as pl
from jax.experimental.pallas import tpu as pltpu
from jax.sharding import PartitionSpec as P


def contract_last(left, right):
    return lax.dot_general(
        left, right, (((1,), (1,)), ((), ())), preferred_element_type=jnp.float32
    )


def contract_first(left, right):
    return lax.dot_general(
        left, right, (((0,), (0,)), ((), ())), preferred_element_type=jnp.float32
    )


def expert_rows(rows_in, cotangent_rows, weight_in, gate_w, up_w, down_w):
    gate_pre = jnp.dot(rows_in, gate_w, preferred_element_type=jnp.float32)
    up_pre = jnp.dot(rows_in, up_w, preferred_element_type=jnp.float32)
    gate_sigmoid = jax.nn.sigmoid(gate_pre)
    activated = gate_pre * gate_sigmoid
    hidden = activated * up_pre
    hidden_raw = contract_last(cotangent_rows, down_w)
    delta_prob = jnp.sum(hidden * hidden_raw, axis=-1).astype(jnp.bfloat16)
    scale_col = weight_in.astype(jnp.float32)[:, None]
    hidden_grad = scale_col * hidden_raw
    up_grad = (hidden_grad * activated).astype(jnp.bfloat16)
    gate_grad = (
        hidden_grad * up_pre * gate_sigmoid * (1.0 + gate_pre * (1.0 - gate_sigmoid))
    ).astype(jnp.bfloat16)
    grad_rows = (contract_last(gate_grad, gate_w) + contract_last(up_grad, up_w)).astype(
        jnp.bfloat16
    )
    scaled_hidden = (scale_col * hidden).astype(jnp.bfloat16)
    return (grad_rows, delta_prob, gate_grad, up_grad, scaled_hidden)


def local(tokens, cotangent, expert_ids, routing, gate_proj, up_proj, down_proj):
    peers = lax.axis_size("ep")
    tok_rows, model_width = tokens.shape
    choose = expert_ids.shape[1]
    assigned = tok_rows * choose
    capacity = assigned // peers + max(1, assigned // (8 * peers))
    total_rows = peers * capacity
    flat_ids = expert_ids.reshape(-1)
    matches = (flat_ids[:, None] == jnp.arange(peers, dtype=jnp.int32)[None, :]).astype(jnp.int32)
    slot_index = jnp.sum(
        (jnp.cumsum(matches, axis=0, dtype=jnp.int32) - matches) * matches, axis=1, dtype=jnp.int32
    )
    target = flat_ids * capacity + slot_index
    owner_row = jnp.arange(assigned, dtype=jnp.int32) // choose
    send_rows = jnp.zeros((total_rows, model_width), jnp.bfloat16).at[target].set(tokens[owner_row])
    send_cotangent = (
        jnp.zeros((total_rows, model_width), jnp.bfloat16).at[target].set(cotangent[owner_row])
    )
    send_weight = jnp.zeros((total_rows,), jnp.bfloat16).at[target].set(routing.reshape(-1))
    send_rows = send_rows.reshape(peers, capacity, model_width)
    send_cotangent = send_cotangent.reshape(peers, capacity, model_width)
    send_weight = send_weight.reshape(peers, capacity)
    gate_w = gate_proj[0]
    up_w = up_proj[0]
    down_w = down_proj[0]
    hidden_width = gate_w.shape[1]
    rows_in = lax.all_to_all(send_rows, "ep", split_axis=0, concat_axis=0, tiled=True)
    cotangent_in = lax.all_to_all(send_cotangent, "ep", split_axis=0, concat_axis=0, tiled=True)
    weight_in = lax.all_to_all(send_weight, "ep", split_axis=0, concat_axis=0, tiled=True)
    count = rows_in.shape[1]
    grad_rows, delta_prob, gate_grad, up_grad, scaled_hidden = expert_rows(
        rows_in.reshape(-1, model_width),
        cotangent_in.reshape(-1, model_width),
        weight_in.reshape(-1),
        gate_w,
        up_w,
        down_w,
    )
    back_rows = lax.all_to_all(
        grad_rows.reshape(peers, count, model_width), "ep", split_axis=0, concat_axis=0, tiled=True
    )
    back_prob = lax.all_to_all(
        delta_prob.reshape(peers, count), "ep", split_axis=0, concat_axis=0, tiled=True
    )
    recv_rows, recv_cotangent, gate_grad, up_grad, scaled_hidden, back_rows, back_prob = (
        rows_in,
        cotangent_in,
        gate_grad.reshape(peers, count, hidden_width),
        up_grad.reshape(peers, count, hidden_width),
        scaled_hidden.reshape(peers, count, hidden_width),
        back_rows,
        back_prob,
    )
    inputs_all = recv_rows.reshape(total_rows, model_width)
    cotangent_all = recv_cotangent.reshape(total_rows, model_width)
    gate_grad = gate_grad.reshape(total_rows, hidden_width)
    up_grad = up_grad.reshape(total_rows, hidden_width)
    scaled_hidden = scaled_hidden.reshape(total_rows, hidden_width)
    grad_gate = contract_first(inputs_all, gate_grad).astype(jnp.bfloat16)[None]
    grad_up = contract_first(inputs_all, up_grad).astype(jnp.bfloat16)[None]
    grad_down = contract_first(scaled_hidden, cotangent_all).astype(jnp.bfloat16)[None]
    back_flat = back_rows.reshape(total_rows, model_width)
    assignment_grad = back_flat[target].astype(jnp.float32).reshape(tok_rows, choose, model_width)
    grad_tokens = jnp.sum(assignment_grad, axis=1).astype(jnp.bfloat16)
    grad_routing = back_prob.reshape(-1)[target].reshape(tok_rows, choose)
    return (grad_tokens, grad_routing, grad_gate, grad_up, grad_down)


LANES = 128


def pick(table, row, column):
    value = jnp.int32(0)
    for r, entries in enumerate(table):
        for s, entry in enumerate(entries):
            value = value + jnp.where((row == r) & (column == s), entry, 0)
    return value


def expert_kernel(
    depth,
    first_rows,
    tokens_ref,
    cotangent_ref,
    ids_ref,
    routing_ref,
    gate_hbm,
    up_hbm,
    down_hbm,
    grad_tokens_ref,
    grad_routing_ref,
    grad_gate_ref,
    grad_up_ref,
    grad_down_ref,
    rows_all,
    partial,
    core_in,
    side_in,
    rise_in,
    fall_in,
    pair_t,
    hidden_t,
    gate_w,
    up_w,
    down_w,
    local_sem,
    gather_send,
    gather_recv,
    core_send,
    core_recv,
    side_send,
    side_recv,
    chain_send,
    chain_recv,
):
    block, width = tokens_ref.shape
    hidden_width = gate_w.shape[1]
    me = lax.axis_index("ep")
    z, y, c = me // 4, (me // 2) % 2, me % 2
    sibling = z * 4 + y * 2 + (1 - c)
    side = z * 4 + (1 - y) * 2 + c
    above, below = me + 4, me - 4
    near = [sorted(range(depth), key=lambda o, r=r: (abs(o - r), o)) for r in range(depth)]
    chain = [
        list(range(r + 1, depth)) + list(range(r - 1, -1, -1))
        if r < depth // 2
        else list(range(r - 1, -1, -1)) + list(range(r + 1, depth))
        for r in range(depth)
    ]
    parts = ((0, first_rows), (first_rows, block - first_rows))

    def at_rows(o, n=1):
        return pl.ds(pl.multiple_of(o * block, block), n * block)

    def local_copies():
        mine = at_rows(me)
        return (
            pltpu.make_async_copy(tokens_ref, rows_all.at[mine, 0:width], local_sem.at[0]),
            pltpu.make_async_copy(
                cotangent_ref, rows_all.at[mine, width : 2 * width], local_sem.at[1]
            ),
            pltpu.make_async_copy(gate_hbm, gate_w, local_sem.at[2]),
            pltpu.make_async_copy(up_hbm, up_w, local_sem.at[3]),
            pltpu.make_async_copy(down_hbm, down_w, local_sem.at[4]),
        )

    def gather_copy(kind, o, way, target):
        start, size = parts[kind]
        where = rows_all.at[pl.ds(pl.multiple_of(o * block + start, 16), size), :]
        return pltpu.make_async_remote_copy(
            src_ref=where,
            dst_ref=where,
            send_sem=gather_send.at[kind, way, o],
            recv_sem=gather_recv.at[kind, o],
            device_id={"ep": target},
            device_id_type=pl.DeviceIdType.MESH,
        )

    def send_along(kind, zo, o):
        @pl.when((zo <= z) & (z < depth - 1))
        def _():
            gather_copy(kind, o, 0, above).start()

        @pl.when((zo >= z) & (z > 0))
        def _():
            gather_copy(kind, o, 1, below).start()

    def arrive(kind, o):
        gather_copy(kind, o, 3, sibling).wait_recv()

    def forward(s):
        zo = pick(near, z, s)
        own = zo * 4 + y * 2 + c
        other = zo * 4 + (1 - y) * 2 + c

        @pl.when(s > 0)
        def _():
            arrive(0, own)

        send_along(0, zo, own)
        gather_copy(0, own, 2, side).start()

        @pl.when(s > 0)
        def _():
            arrive(1, own)

        send_along(1, zo, own)

        @pl.when(s == 0)
        def _():
            gather_copy(1, own, 2, side).start()

        gather_copy(0, own, 3, sibling).start()
        gather_copy(1, own, 3, sibling).start()
        arrive(1, other)
        send_along(1, zo, other)
        gather_copy(1, other, 3, sibling).start()

    def core_copy(zo, yo):
        return pltpu.make_async_remote_copy(
            src_ref=partial.at[at_rows(zo * 4 + yo * 2 + (1 - c)), :],
            dst_ref=core_in.at[at_rows(zo * 2 + yo), :],
            send_sem=core_send.at[zo * 2 + yo],
            recv_sem=core_recv.at[zo * 2 + yo],
            device_id={"ep": sibling},
            device_id_type=pl.DeviceIdType.MESH,
        )

    def side_copy(zo):
        return pltpu.make_async_remote_copy(
            src_ref=partial.at[at_rows(zo * 4 + (1 - y) * 2 + c), :],
            dst_ref=side_in.at[at_rows(zo), :],
            send_sem=side_send.at[zo],
            recv_sem=side_recv.at[zo],
            device_id={"ep": side},
            device_id_type=pl.DeviceIdType.MESH,
        )

    def quarter_rows(o, quarter):
        start = o * block + quarter * (block // 4)
        return pl.ds(pl.multiple_of(start, block // 4), block // 4)

    def chain_copy(zo, way, target, quarter):
        return pltpu.make_async_remote_copy(
            src_ref=partial.at[quarter_rows(zo * 4 + y * 2 + c, quarter), :],
            dst_ref=(rise_in if way == 0 else fall_in).at[quarter_rows(zo, quarter), :],
            send_sem=chain_send.at[way, zo, quarter],
            recv_sem=chain_recv.at[way, zo, quarter],
            device_id={"ep": target},
            device_id_type=pl.DeviceIdType.MESH,
        )

    def add_into(o, source, at):
        total = partial[at_rows(o), :].astype(jnp.float32) + source[at_rows(at), :].astype(
            jnp.float32
        )
        partial[at_rows(o), :] = total.astype(jnp.bfloat16)

    def compute(s):
        zo = pick(near, z, s)
        other = zo * 4 + (1 - y) * 2 + c
        arrive(0, other)
        gather_copy(0, other, 3, sibling).start()
        for kind in (0, 1):
            for yo in (0, 1):
                arrive(kind, zo * 4 + yo * 2 + (1 - c))

        @pl.when(s == 0)
        def _():
            for copy in local_copies()[2:]:
                copy.wait()

        @pl.loop(0, 2)
        def _(yo):
            start = pl.multiple_of((zo * 4 + yo * 2) * block, 2 * block)
            rows = pl.ds(start, 2 * block)
            lane = lax.broadcasted_iota(jnp.int32, (2 * block, LANES), 1)
            x = rows_all[rows, 0:width]
            gate_pre = jnp.dot(x, gate_w[...], preferred_element_type=jnp.float32)
            up_pre = jnp.dot(x, up_w[...], preferred_element_type=jnp.float32)
            hidden_raw = contract_last(rows_all[rows, width : 2 * width], down_w[...])
            weights = rows_all[rows, 2 * width : 2 * width + LANES].astype(jnp.float32)
            scale_col = jnp.sum(jnp.where(lane == me, weights, 0.0), axis=1, keepdims=True)
            gate_sigmoid = jax.nn.sigmoid(gate_pre)
            activated = gate_pre * gate_sigmoid
            hidden = activated * up_pre
            delta_prob = jnp.sum(hidden * hidden_raw, axis=1, keepdims=True)
            partial[rows, width : width + LANES] = jnp.where(lane == me, delta_prob, 0.0).astype(
                jnp.bfloat16
            )
            hidden_grad = scale_col * hidden_raw
            up_grad = hidden_grad * activated
            gate_grad = (
                hidden_grad * up_pre * gate_sigmoid * (1.0 + gate_pre * (1.0 - gate_sigmoid))
            )
            pair_t[0:hidden_width, rows] = gate_grad.T.astype(jnp.bfloat16)
            pair_t[hidden_width : 2 * hidden_width, rows] = up_grad.T.astype(jnp.bfloat16)
            hidden_t[:, rows] = (scale_col * hidden).T.astype(jnp.bfloat16)
            up_grad = up_grad.astype(jnp.bfloat16)
            gate_grad = gate_grad.astype(jnp.bfloat16)
            for tile in range(0, width, 512):
                span = slice(tile, tile + 512)
                partial[rows, span] = (
                    contract_last(gate_grad, gate_w[span, :])
                    + contract_last(up_grad, up_w[span, :])
                ).astype(jnp.bfloat16)
            core_copy(zo, yo).start()

    def sum_core(s):
        zo = pick(near, z, s)
        core_copy(zo, 1 - y).wait_recv()
        add_into(zo * 4 + (1 - y) * 2 + c, core_in, zo * 2 + (1 - y))
        side_copy(zo).start()
        core_copy(zo, y).wait_recv()
        add_into(zo * 4 + y * 2 + c, core_in, zo * 2 + y)

    def sum_side(s):
        zo = pick(near, z, s)
        side_copy(zo).wait_recv()
        add_into(zo * 4 + y * 2 + c, side_in, zo)

    def sum_chain(s):
        zo = pick(chain, z, s)
        own = zo * 4 + y * 2 + c

        def pass_on(way, target, inner, source):
            @pl.loop(0, 4)
            def _(quarter):
                @pl.when(inner)
                def _():
                    chain_copy(zo, way, target, quarter).wait_recv()
                    rows = quarter_rows(own, quarter)
                    total = partial[rows, :].astype(jnp.float32) + source[
                        quarter_rows(zo, quarter), :
                    ].astype(jnp.float32)
                    partial[rows, :] = total.astype(jnp.bfloat16)

                chain_copy(zo, way, target, quarter).start()

        @pl.when(zo > z)
        def _():
            pass_on(0, above, z > 0, rise_in)

        @pl.when(zo < z)
        def _():
            pass_on(1, below, z < depth - 1, fall_in)

    tile_width = 256

    def weight_grads(low, high):
        @pl.loop(low, high)
        def _(tile):
            start = pl.multiple_of(tile * tile_width, tile_width)
            span = pl.ds(start, tile_width)
            pair = jnp.dot(
                pair_t[...], rows_all[:, span], preferred_element_type=jnp.float32
            ).astype(jnp.bfloat16)
            grad_gate_ref[:, span] = pair[:hidden_width]
            grad_up_ref[:, span] = pair[hidden_width:]
            grad_down_ref[:, span] = jnp.dot(
                hidden_t[...],
                rows_all[:, pl.ds(pl.multiple_of(start + width, tile_width), tile_width)],
                preferred_element_type=jnp.float32,
            ).astype(jnp.bfloat16)

    for copy in local_copies():
        copy.start()
    barrier = pltpu.get_barrier_semaphore()
    for target in (sibling, side):
        pl.semaphore_signal(
            barrier, inc=1, device_id={"ep": target}, device_id_type=pl.DeviceIdType.MESH
        )

    @pl.when(z < depth - 1)
    def _():
        pl.semaphore_signal(
            barrier, inc=1, device_id={"ep": above}, device_id_type=pl.DeviceIdType.MESH
        )

    @pl.when(z > 0)
    def _():
        pl.semaphore_signal(
            barrier, inc=1, device_id={"ep": below}, device_id_type=pl.DeviceIdType.MESH
        )

    ends = jnp.where(z > 0, 1, 0) + jnp.where(z < depth - 1, 1, 0)
    pl.semaphore_wait(barrier, 2 + ends)
    lane = lax.broadcasted_iota(jnp.int32, (block, LANES), 1)
    choose = ids_ref.shape[1]
    weights = jnp.zeros((block, LANES), jnp.float32)
    for k in range(choose):
        weights = weights + jnp.where(
            lane == ids_ref[:, k : k + 1], routing_ref[:, k : k + 1].astype(jnp.float32), 0.0
        )
    rows_all[at_rows(me), 2 * width : 2 * width + LANES] = weights.astype(jnp.bfloat16)
    for copy in local_copies()[:2]:
        copy.wait()

    edge = (z == 0) | (z == depth - 1)
    last = depth - 1

    @pl.loop(0, depth + 2)
    def _(s):
        @pl.when(s < depth)
        def _():
            forward(s)

        @pl.when((s >= 1) & (s <= depth))
        def _():
            compute(s - 1)
            sum_core(s - 1)

        @pl.when(s == depth)
        def _():
            weight_grads(0, 4)

        @pl.when(s >= 2)
        def _():
            sum_side(s - 2)

        @pl.when((s >= 3) & edge)
        def _():
            sum_chain(s - 3)

        @pl.when((s == depth) & (z > 0) & (z < last))
        def _():
            sum_chain(0)

    @pl.when((z > 0) & (z < last))
    def _():
        @pl.loop(1, last)
        def _(s):
            sum_chain(s)

    weight_grads(4, width // tile_width)

    @pl.when(z > 0)
    def _():
        chain_copy(z, 0, above, 0).wait_recv()
        chain_copy(z, 0, above, 1).wait_recv()
        chain_copy(z, 0, above, 2).wait_recv()
        chain_copy(z, 0, above, 3).wait_recv()

    @pl.when(z == 0)
    def _():
        rise_in[at_rows(z), :] = jnp.zeros((block, width + LANES), jnp.bfloat16)

    @pl.when(z < depth - 1)
    def _():
        chain_copy(z, 1, below, 0).wait_recv()
        chain_copy(z, 1, below, 1).wait_recv()
        chain_copy(z, 1, below, 2).wait_recv()
        chain_copy(z, 1, below, 3).wait_recv()

    @pl.when(z == depth - 1)
    def _():
        fall_in[at_rows(z), :] = jnp.zeros((block, width + LANES), jnp.bfloat16)

    total = (
        partial[at_rows(me), :].astype(jnp.float32)
        + rise_in[at_rows(z), :].astype(jnp.float32)
        + fall_in[at_rows(z), :].astype(jnp.float32)
    )
    grad_tokens_ref[...] = total[:, :width].astype(jnp.bfloat16)
    probs = total[:, width:]
    found = jnp.zeros((block, LANES), jnp.float32)
    for k in range(choose):
        value = jnp.sum(
            jnp.where(lane == ids_ref[:, k : k + 1], probs, 0.0), axis=1, keepdims=True
        )
        found = found + jnp.where(lane == k, value, 0.0)
    grad_routing_ref[...] = found.astype(jnp.bfloat16)

    @pl.loop(0, depth)
    def _(zo):
        own = zo * 4 + y * 2 + c
        other = zo * 4 + (1 - y) * 2 + c
        for kind, o in ((0, own), (1, own), (1, other)):
            @pl.when((zo <= z) & (z < depth - 1))
            def _(kind=kind, o=o):
                gather_copy(kind, o, 0, above).wait_send()

            @pl.when((zo >= z) & (z > 0))
            def _(kind=kind, o=o):
                gather_copy(kind, o, 1, below).wait_send()

        gather_copy(0, own, 2, side).wait_send()

        @pl.when(zo == z)
        def _():
            gather_copy(1, own, 2, side).wait_send()

        for kind in (0, 1):
            for o in (own, other):
                gather_copy(kind, o, 3, sibling).wait_send()
        core_copy(zo, 0).wait_send()
        core_copy(zo, 1).wait_send()
        side_copy(zo).wait_send()

        @pl.when(zo > z)
        def _():
            chain_copy(zo, 0, above, 0).wait_send()
            chain_copy(zo, 0, above, 1).wait_send()
            chain_copy(zo, 0, above, 2).wait_send()
            chain_copy(zo, 0, above, 3).wait_send()

        @pl.when(zo < z)
        def _():
            chain_copy(zo, 1, below, 0).wait_send()
            chain_copy(zo, 1, below, 1).wait_send()
            chain_copy(zo, 1, below, 2).wait_send()
            chain_copy(zo, 1, below, 3).wait_send()


def dense_local(tokens, cotangent, expert_ids, routing, gate_proj, up_proj, down_proj):
    peers = lax.axis_size("ep")
    depth = peers // 4
    block, width = tokens.shape
    choose = expert_ids.shape[1]
    hidden_width = gate_proj.shape[2]
    total = peers * block
    first_rows = block * 6 // 8
    bf16 = jnp.bfloat16
    vmem = pl.BlockSpec(memory_space=pltpu.VMEM)
    anywhere = pl.BlockSpec(memory_space=pl.ANY)
    dma = pltpu.SemaphoreType.DMA
    grad_tokens, grad_routing, grad_gate, grad_up, grad_down = pl.pallas_call(
        functools.partial(expert_kernel, depth, first_rows),
        out_shape=(
            jax.ShapeDtypeStruct((block, width), bf16),
            jax.ShapeDtypeStruct((block, LANES), bf16),
            jax.ShapeDtypeStruct((hidden_width, width), bf16),
            jax.ShapeDtypeStruct((hidden_width, width), bf16),
            jax.ShapeDtypeStruct((hidden_width, width), bf16),
        ),
        in_specs=[anywhere, anywhere, vmem, vmem, anywhere, anywhere, anywhere],
        out_specs=(vmem, vmem, vmem, vmem, vmem),
        scratch_shapes=[
            pltpu.VMEM((total, 2 * width + LANES), bf16),
            pltpu.VMEM((total, width + LANES), bf16),
            pltpu.VMEM((total // 2, width + LANES), bf16),
            pltpu.VMEM((total // 4, width + LANES), bf16),
            pltpu.VMEM((total // 4, width + LANES), bf16),
            pltpu.VMEM((total // 4, width + LANES), bf16),
            pltpu.VMEM((2 * hidden_width, total), bf16),
            pltpu.VMEM((hidden_width, total), bf16),
            pltpu.VMEM((width, hidden_width), bf16),
            pltpu.VMEM((width, hidden_width), bf16),
            pltpu.VMEM((hidden_width, width), bf16),
            dma((5,)),
            dma((2, 4, peers)),
            dma((2, peers)),
            dma((2 * depth,)),
            dma((2 * depth,)),
            dma((depth,)),
            dma((depth,)),
            dma((2, depth, 4)),
            dma((2, depth, 4)),
        ],
        compiler_params=pltpu.CompilerParams(
            collective_id=0, has_side_effects=True, vmem_limit_bytes=62 << 20
        ),
        cost_estimate=pl.CostEstimate(
            flops=16 * total * width * hidden_width,
            bytes_accessed=20 * width * hidden_width,
            transcendentals=total * hidden_width,
        ),
    )(tokens, cotangent, expert_ids, routing, gate_proj[0], up_proj[0], down_proj[0])
    return (
        grad_tokens,
        grad_routing[:, :choose],
        grad_gate.T[None],
        grad_up.T[None],
        grad_down[None],
    )


def solution(mesh):
    return jax.shard_map(
        dense_local if mesh.shape["ep"] == 16 else local,
        mesh=mesh,
        in_specs=(
            P(("grp", "ep"), None),
            P(("grp", "ep"), None),
            P(("grp", "ep"), None),
            P(("grp", "ep"), None),
            P("ep", None, None),
            P("ep", None, None),
            P("ep", None, None),
        ),
        out_specs=(
            P(("grp", "ep"), None),
            P(("grp", "ep"), None),
            P(("grp", "ep"), None, None),
            P(("grp", "ep"), None, None),
            P(("grp", "ep"), None, None),
        ),
        check_vma=False,
    )
```
